128 devices in a mesh: ctx: 8 (over x, y_hi), head: 16 (over z, y_lo, core).
Axes of the slice: x: 4, y: 4 (y_hi: 2, y_lo: 2; y = y_hi * 2 + y_lo), z: 4, core: 2. Of those that a mesh axis runs over, the one named last changes fastest.
Arguments:
- query: bfloat16 [131072, 1024], P(('ctx', 'head')), may hold values from -7 to 7
- key: bfloat16 [131072, 1024], P(('ctx', 'head')), may hold values from -7 to 7
- value: bfloat16 [131072, 1024], P(('ctx', 'head')), may hold values from -6 to 6
- pattern: int32 [16, 1024, 12], P('head', 'ctx'), may hold values from 0 to 1023, as said below
Outputs:
- attended: bfloat16 [131072, 1024], P(('ctx', 'head'))
The draws below stay inside these ranges and needn't reach their ends.
Inputs may be any that keep to these rules, and one draw needn't show every extreme that they name: pattern[h, b] holds 12 different key block numbers, the first of them b itself. Cut the blocks into aligned groups of 128; for each head and each group, the key blocks read by the group's query blocks that lie outside the group are exactly 2 different blocks from each other group.
All inputs are finite; a program needn't handle non-finite values.
Results may differ from the reference program's by a relative error of at most 0.0047.
Values may be sent and summed in bfloat16 or wider, within the bound.
No kernel may reach another device: no remote copies, remote signals or barrier semaphores. Data moves between devices by JAX's collectives and lax.ppermute only.
A program may use at most 192 MiB of HBM per device.

```python
import math
import jax
import jax.numpy as jnp
from jax import lax

HEADS = 16
DH = 64
BLK = 128
KPER = 12
PMOST = 2
SEQ = 131072
QB = 128
D = 1024


def draw_query(key, part):
    key = jax.random.fold_in(key, 3)
    base_vals = jnp.clip(jax.random.normal(key, (SEQ, HEADS * DH), jnp.float32), -6.0, 6.0)
    return base_vals.astype(jnp.bfloat16)


def draw_key(key, part):
    key = jax.random.fold_in(key, 7)
    base_vals = jnp.clip(jax.random.normal(key, (SEQ, HEADS * DH), jnp.float32), -6.0, 6.0)
    return base_vals.astype(jnp.bfloat16)


def draw_pattern(key, part):
    key = jax.random.fold_in(key, 5)
    noise_key, pick_key = jax.random.split(key)
    blocks = SEQ // BLK
    ranges = blocks // QB
    remote = PMOST * (ranges - 1)
    random_rank = jax.random.randint(pick_key, (HEADS, ranges, ranges - 1, QB), 0, 65536) * QB + jnp.arange(QB, dtype=jnp.int32)
    picked_pos = lax.top_k(random_rank, PMOST)[1].astype(jnp.int32)
    range_ids = jnp.arange(ranges, dtype=jnp.int32)[:, None]
    steps_ahead = jnp.arange(1, ranges, dtype=jnp.int32)[None, :]
    other_range = (range_ids + steps_ahead) % ranges
    remote_blocks = (other_range[None, :, :, None] * QB + picked_pos).reshape(HEADS, ranges, remote)
    col_ids = jnp.arange(blocks, dtype=jnp.int32)
    member = jnp.any(remote_blocks[:, :, :, None] == col_ids, axis=2)
    member_rows = jnp.repeat(member, QB, axis=1)
    filler = -jnp.ones((HEADS, ranges, QB - remote), jnp.int32)
    forced_col = jnp.concatenate([remote_blocks, filler], axis=2).reshape(HEADS, blocks)
    row_ids = col_ids[:, None]
    col_row = col_ids[None, :]
    same_range = row_ids // QB == col_row // QB
    near_band = jnp.logical_and(jnp.abs(row_ids - col_row) <= 2, same_range).astype(jnp.int32)
    noise_vals = jax.random.randint(noise_key, (HEADS, blocks, blocks), 0, 1024)
    base_score = (noise_vals + 300 * near_band[None]) * blocks + col_row[None]
    final_score = jnp.where(jnp.logical_or(same_range[None], member_rows), base_score, -1 - col_row[None])
    final_score = jnp.where(col_row[None] == forced_col[:, :, None], 268435456 + col_row[None], final_score)
    final_score = jnp.where((row_ids == col_row)[None], 536870912, final_score)
    return lax.top_k(final_score, KPER)[1].astype(jnp.int32)


def shard_levels(rng, dims, shards, smallest, top_value):
    factor_of = 1.0
    for position, blocks in shards:
        draws = jax.random.uniform(jax.random.fold_in(jax.random.fold_in(rng, 6), position), (blocks,), jnp.float32, smallest / len(shards), top_value / len(shards))
        factor_of = factor_of * jnp.repeat(jnp.exp(draws), dims[position] // blocks).reshape((-1,) + (1,) * (len(dims) - 1 - position))
    return factor_of


def normal_values(rng, dims, width, reach, pieces=(), kind=jnp.bfloat16):
    array = width * jax.random.normal(rng, dims, jnp.float32)
    if pieces:
        array = array * shard_levels(rng, dims, pieces, -0.22, 0.18)
    return jnp.clip(array, -reach, reach).astype(kind)


def setup_inputs(seed: int = 0) -> dict:
    splits = jax.random.split(jax.random.key(seed), 5)
    return {
        "query": draw_query(jax.random.fold_in(splits[4], 71), 0),
        "key": draw_key(jax.random.fold_in(splits[4], 71), 0),
        "value": normal_values(splits[2], (SEQ, D), 1.0, 6.0, ((0, 128),)),
        "pattern": draw_pattern(jax.random.fold_in(splits[4], 71), 0),
    }


def reference(query, key, value, pattern):
    blocks = SEQ // BLK
    group_size = math.gcd(blocks, 16)
    ngroups = blocks // group_size
    score_scale = DH ** -0.5

    def one_head(head_idx):
        q_head = lax.dynamic_slice_in_dim(query, head_idx * DH, DH, 1).reshape(ngroups, group_size, BLK, DH)
        k_head = lax.dynamic_slice_in_dim(key, head_idx * DH, DH, 1).reshape(blocks, BLK, DH)
        v_head = lax.dynamic_slice_in_dim(value, head_idx * DH, DH, 1).reshape(blocks, BLK, DH)
        pat_head = pattern[head_idx].reshape(ngroups, group_size, KPER)

        def one_group(inputs):
            q_grp, pat_grp = inputs
            k_grp = k_head[pat_grp].astype(jnp.float32)
            v_grp = v_head[pat_grp].astype(jnp.float32)
            scores = jnp.einsum("gqd,gjkd->gqjk", q_grp.astype(jnp.float32), k_grp) * score_scale
            row_top = jnp.max(scores, axis=(2, 3), keepdims=True)
            exp_scores = jnp.exp(scores - row_top)
            row_total = jnp.sum(exp_scores, axis=(2, 3))
            rounded = lax.optimization_barrier(exp_scores.astype(jnp.bfloat16)).astype(jnp.float32)
            summed = jnp.einsum("gqjk,gjkd->gqd", rounded, v_grp)
            return (summed / row_total[..., None]).astype(jnp.bfloat16)

        return lax.map(one_group, (q_head, pat_head))

    heads_out = lax.map(one_head, jnp.arange(HEADS, dtype=jnp.int32))
    heads_out = heads_out.reshape(HEADS, SEQ, DH)
    return jnp.transpose(heads_out, (1, 0, 2)).reshape(SEQ, HEADS * DH)
```

```python
import functools

import jax
import jax.numpy as jnp
from jax import lax
from jax.experimental import pallas as pl
from jax.experimental.pallas import tpu as pltpu
from jax.sharding import PartitionSpec as P

DH = 64
BLK = 128
KPER = 12
PMOST = 2
LANES = 2 * DH
NT = (((1,), (1,)), ((), ()))
NN = (((1,), (0,)), ((), ()))
VMEM_LIMIT = 48 * 1024 * 1024


def pack_kv(key, value):
    tok, width = key.shape

    def body(k_ref, v_ref, o_ref):
        k, v = k_ref[...], v_ref[...]
        o_ref[0] = jnp.concatenate([k[:, :DH], v[:, :DH]], axis=1)
        o_ref[1] = jnp.concatenate([k[:, DH:], v[:, DH:]], axis=1)

    spec = pl.BlockSpec((tok, LANES), lambda c: (0, c))
    return pl.pallas_call(
        body,
        grid=(width // LANES,),
        in_specs=[spec, spec],
        out_specs=pl.BlockSpec((2, tok, LANES), lambda c: (c, 0, 0)),
        out_shape=jax.ShapeDtypeStruct((width // DH, tok, LANES), jnp.bfloat16),
        cost_estimate=pl.CostEstimate(flops=0, bytes_accessed=8 * tok * width, transcendentals=0),
        name="pack_kv",
    )(key, value)


def pack_q(query, chunks):
    tok, width = query.shape
    pairs = tok // (2 * BLK)
    per = pairs // chunks

    def body(q_ref, *outs):
        for p in range(pairs):
            o_ref = outs[p // per]
            a = q_ref[2 * p * BLK : (2 * p + 1) * BLK, :] * jnp.bfloat16(0.125)
            b = q_ref[(2 * p + 1) * BLK : (2 * p + 2) * BLK, :] * jnp.bfloat16(0.125)
            o_ref[0, p % per] = jnp.concatenate([a[:, :DH], b[:, :DH]], axis=1)
            o_ref[1, p % per] = jnp.concatenate([a[:, DH:], b[:, DH:]], axis=1)

    shape = jax.ShapeDtypeStruct((width // DH, per, BLK, LANES), jnp.bfloat16)
    return pl.pallas_call(
        body,
        grid=(width // LANES,),
        in_specs=[pl.BlockSpec((tok, LANES), lambda c: (0, c))],
        out_specs=[pl.BlockSpec((2, per, BLK, LANES), lambda c: (c, 0, 0, 0))] * chunks,
        out_shape=[shape] * chunks,
        cost_estimate=pl.CostEstimate(flops=0, bytes_accessed=4 * tok * width, transcendentals=0),
        name="pack_q",
    )(query)


def pick_blocks(kv_blocks, wanted):
    count = wanted.shape[0]

    def body(w_ref, kv_ref, o_ref, sem):
        copies = [
            pltpu.make_async_copy(kv_ref.at[w_ref[i]], o_ref.at[i], sem.at[i]) for i in range(count)
        ]
        for c in copies:
            c.start()
        for c in copies:
            c.wait()

    return pl.pallas_call(
        body,
        in_specs=[
            pl.BlockSpec(memory_space=pltpu.SMEM),
            pl.BlockSpec(memory_space=pl.ANY),
        ],
        out_specs=pl.BlockSpec(memory_space=pl.ANY),
        out_shape=jax.ShapeDtypeStruct((count,) + kv_blocks.shape[1:], jnp.bfloat16),
        scratch_shapes=[pltpu.SemaphoreType.DMA((count,))],
        cost_estimate=pl.CostEstimate(
            flops=0, bytes_accessed=count * BLK * LANES * 4, transcendentals=0
        ),
        name="pick_blocks",
    )(wanted, kv_blocks)


def attend(table_index, q_pairs, kv_local, kv_remote, first_block, per_source):
    sources, per = q_pairs.shape[:2]
    pairs = sources * per
    nlocal, nremote = kv_local.shape[0], kv_remote.shape[0]
    q_flat = q_pairs.reshape(pairs, BLK, LANES)

    def body(idx_ref, q_ref, loc_ref, rem_ref, o_ref, tab, s_buf, m_buf, sems):
        c0 = pltpu.make_async_copy(loc_ref, tab.at[pl.ds(0, nlocal)], sems.at[0])
        c1 = pltpu.make_async_copy(rem_ref, tab.at[pl.ds(nlocal, nremote)], sems.at[1])
        c0.start()
        c1.start()
        c0.wait()
        c1.wait()
        zeros = jnp.zeros((BLK, DH), jnp.bfloat16)

        def entry(pair, half):
            block = (pair // per) * per_source + first_block + 2 * (pair % per) + half
            return block * KPER

        def keys_of(base, jj):
            return jnp.concatenate(
                [tab[idx_ref[base + 2 * jj]], tab[idx_ref[base + 2 * jj + 1]]], axis=0
            )

        def score(pair, half):
            base = entry(pair, half)
            q = jnp.concatenate([q_ref[pair, :, half * DH : (half + 1) * DH], zeros], axis=1)
            top = None
            for jj in range(KPER // 2):
                s = lax.dot_general(q, keys_of(base, jj), NT, preferred_element_type=jnp.float32)
                s_buf[half, :, jj * 2 * BLK : (jj + 1) * 2 * BLK] = s
                both = jnp.maximum(s[:, :BLK], s[:, BLK:])
                top = both if top is None else jnp.maximum(top, both)
            m_buf[half] = jnp.broadcast_to(jnp.max(top, axis=1, keepdims=True), (BLK, LANES))

        def finish(pair, half):
            base = entry(pair, half)
            top = m_buf[half]
            top2 = jnp.concatenate([top, top], axis=1)
            total, acc = None, None
            for jj in range(KPER // 2):
                p = jnp.exp(s_buf[half, :, jj * 2 * BLK : (jj + 1) * 2 * BLK] - top2)
                both = p[:, :BLK] + p[:, BLK:]
                total = both if total is None else total + both
                part = lax.dot_general(
                    p.astype(jnp.bfloat16),
                    keys_of(base, jj),
                    NN,
                    preferred_element_type=jnp.float32,
                )
                acc = part if acc is None else acc + part
            total = jnp.sum(total, axis=1, keepdims=True)
            return (acc[:, DH:] / total).astype(jnp.bfloat16)

        score(0, 0)

        def step(i, carry):
            score(i, 1)
            a = finish(i, 0)
            score(jnp.minimum(i + 1, pairs - 1), 0)
            b = finish(i, 1)
            o_ref[i] = jnp.concatenate([a, b], axis=1)
            return carry

        lax.fori_loop(0, pairs, step, 0)

    out = pl.pallas_call(
        body,
        in_specs=[
            pl.BlockSpec(memory_space=pltpu.SMEM),
            pl.BlockSpec(memory_space=pltpu.VMEM),
            pl.BlockSpec(memory_space=pl.ANY),
            pl.BlockSpec(memory_space=pl.ANY),
        ],
        out_specs=pl.BlockSpec(memory_space=pltpu.VMEM),
        out_shape=jax.ShapeDtypeStruct((pairs, BLK, LANES), jnp.bfloat16),
        scratch_shapes=[
            pltpu.VMEM((nlocal + nremote, BLK, LANES), jnp.bfloat16),
            pltpu.VMEM((2, BLK, KPER * BLK), jnp.float32),
            pltpu.VMEM((2, BLK, LANES), jnp.float32),
            pltpu.SemaphoreType.DMA((2,)),
        ],
        compiler_params=pltpu.CompilerParams(vmem_limit_bytes=VMEM_LIMIT),
        cost_estimate=pl.CostEstimate(
            flops=pairs * 2 * KPER * BLK * BLK * LANES * 4,
            bytes_accessed=(nlocal + nremote + 2 * pairs) * BLK * LANES * 2,
            transcendentals=pairs * 2 * KPER * BLK * BLK,
        ),
        name="attend",
    )(table_index, q_flat, kv_local, kv_remote)
    return out.reshape(sources, per, BLK, LANES)


def unpack(o_pairs, tok, width, first_pair, into):
    heads, per = o_pairs.shape[:2]
    rows = per * 2 * BLK

    def body(o_ref, *rest):
        out_ref = rest[-1]
        for p in range(per):
            even, odd = o_ref[0, p], o_ref[1, p]
            out_ref[2 * p * BLK : (2 * p + 1) * BLK, :] = jnp.concatenate(
                [even[:, :DH], odd[:, :DH]], axis=1
            )
            out_ref[(2 * p + 1) * BLK : (2 * p + 2) * BLK, :] = jnp.concatenate(
                [even[:, DH:], odd[:, DH:]], axis=1
            )

    row_block = first_pair // per
    in_specs = [pl.BlockSpec((2, per, BLK, LANES), lambda c: (c, 0, 0, 0))]
    args = [o_pairs]
    if into is not None:
        in_specs.append(pl.BlockSpec(memory_space=pl.ANY))
        args.append(into)
    return pl.pallas_call(
        body,
        grid=(width // LANES,),
        in_specs=in_specs,
        out_specs=pl.BlockSpec((rows, LANES), lambda c: (row_block, c)),
        out_shape=jax.ShapeDtypeStruct((tok, width), jnp.bfloat16),
        input_output_aliases={1: 0} if into is not None else {},
        cost_estimate=pl.CostEstimate(flops=0, bytes_accessed=4 * rows * width, transcendentals=0),
        name="unpack",
    )(*args)


def across(x, axis):
    return lax.all_to_all(x, axis, split_axis=0, concat_axis=0, tiled=True)


def on_device(chunks, query, key, value, pattern):
    tok, width = query.shape
    sources = lax.axis_size("head")
    ranges = lax.axis_size("ctx")
    own = lax.axis_index("ctx")
    per_source = tok // BLK
    count = sources * per_source

    kv_send = pack_kv(key, value)
    kv_blocks = across(kv_send, "head").reshape(count, BLK, LANES)
    q_send = pack_q(query, chunks)

    rows = pattern[0]
    owner, pos = rows // count, rows % count
    of_range = owner[None] == jnp.arange(ranges, dtype=jnp.int32)[:, None, None]
    low = jnp.min(jnp.where(of_range, pos[None], count - 1), axis=(1, 2))
    high = jnp.max(jnp.where(of_range, pos[None], 0), axis=(1, 2))
    wanted = jnp.stack([low, high], axis=1)
    slot = jnp.sum(jnp.where(of_range, (pos[None] != low[:, None, None]).astype(jnp.int32), 0), axis=0)
    table_index = jnp.where(owner == own, pos, count + owner * PMOST + slot).reshape(-1)
    asked = lax.all_gather(wanted, "ctx", axis=0)
    asked = lax.dynamic_index_in_dim(asked, own, axis=1, keepdims=False).reshape(-1)

    picked = pick_blocks(kv_blocks, asked)
    remote = across(picked.reshape(ranges, PMOST * BLK, LANES), "ctx")
    remote = remote.reshape(ranges * PMOST, BLK, LANES)

    out = None
    per = per_source // (2 * chunks)
    for c in range(chunks):
        q_pairs = across(q_send[c], "head")
        o_pairs = attend(table_index, q_pairs, kv_blocks, remote, 2 * per * c, per_source)
        o_pairs = across(o_pairs, "head")
        out = unpack(o_pairs, tok, width, per * c, out)
    return out


def solution(mesh):
    placed = (
        P(("ctx", "head"), None),
        P(("ctx", "head"), None),
        P(("ctx", "head"), None),
        P("head", "ctx", None),
    )
    return jax.shard_map(
        functools.partial(on_device, 2),
        mesh=mesh,
        in_specs=placed,
        out_specs=P(("ctx", "head"), None),
        check_vma=False,
    )
```

```python
import functools

import jax
import jax.numpy as jnp
from jax import lax
from jax.experimental import pallas as pl
from jax.experimental.pallas import tpu as pltpu
from jax.sharding import PartitionSpec as P

DH = 64
BLK = 128
KPER = 12
PMOST = 2
LANES = 2 * DH
NT = (((1,), (1,)), ((), ()))
NN = (((1,), (0,)), ((), ()))
VMEM_LIMIT = 48 * 1024 * 1024


def pack_kv(key, value):
    tok, width = key.shape
    rows = tok // 2

    def body(k_ref, v_ref, o_ref):
        for c in range(width // LANES):
            k = k_ref[:, c * LANES : (c + 1) * LANES]
            v = v_ref[:, c * LANES : (c + 1) * LANES]
            o_ref[2 * c] = jnp.concatenate([k[:, :DH], v[:, :DH]], axis=1)
            o_ref[2 * c + 1] = jnp.concatenate([k[:, DH:], v[:, DH:]], axis=1)

    spec = pl.BlockSpec((rows, width), lambda i: (i, 0))
    return pl.pallas_call(
        body,
        grid=(tok // rows,),
        in_specs=[spec, spec],
        out_specs=pl.BlockSpec((width // DH, rows, LANES), lambda i: (0, i, 0)),
        out_shape=jax.ShapeDtypeStruct((width // DH, tok, LANES), jnp.bfloat16),
        compiler_params=pltpu.CompilerParams(vmem_limit_bytes=VMEM_LIMIT),
        cost_estimate=pl.CostEstimate(flops=0, bytes_accessed=8 * tok * width, transcendentals=0),
        name="pack_kv",
    )(key, value)


def pack_q(query, first_pair, per):
    width = query.shape[1]
    rows = per * 2 * BLK
    row_block = first_pair // per

    def body(q_ref, o_ref):
        for p in range(per):
            for c in range(width // LANES):
                cols = slice(c * LANES, (c + 1) * LANES)
                a = q_ref[2 * p * BLK : (2 * p + 1) * BLK, cols] * jnp.bfloat16(0.125)
                b = q_ref[(2 * p + 1) * BLK : (2 * p + 2) * BLK, cols] * jnp.bfloat16(0.125)
                o_ref[2 * c, p] = jnp.concatenate([a[:, :DH], b[:, :DH]], axis=1)
                o_ref[2 * c + 1, p] = jnp.concatenate([a[:, DH:], b[:, DH:]], axis=1)

    return pl.pallas_call(
        body,
        grid=(1,),
        in_specs=[pl.BlockSpec((rows, width), lambda i: (row_block, 0))],
        out_specs=pl.BlockSpec((width // DH, per, BLK, LANES), lambda i: (0, 0, 0, 0)),
        out_shape=jax.ShapeDtypeStruct((width // DH, per, BLK, LANES), jnp.bfloat16),
        cost_estimate=pl.CostEstimate(flops=0, bytes_accessed=4 * rows * width, transcendentals=0),
        name="pack_q",
    )(query)


def pick_blocks(kv_blocks, wanted):
    count = wanted.shape[0]

    def body(w_ref, kv_ref, o_ref, sem):
        copies = [
            pltpu.make_async_copy(kv_ref.at[w_ref[i]], o_ref.at[i], sem.at[i]) for i in range(count)
        ]
        for c in copies:
            c.start()
        for c in copies:
            c.wait()

    return pl.pallas_call(
        body,
        in_specs=[
            pl.BlockSpec(memory_space=pltpu.SMEM),
            pl.BlockSpec(memory_space=pl.ANY),
        ],
        out_specs=pl.BlockSpec(memory_space=pltpu.VMEM),
        out_shape=jax.ShapeDtypeStruct((count,) + kv_blocks.shape[1:], jnp.bfloat16),
        scratch_shapes=[pltpu.SemaphoreType.DMA((count,))],
        cost_estimate=pl.CostEstimate(
            flops=0, bytes_accessed=count * BLK * LANES * 4, transcendentals=0
        ),
        name="pick_blocks",
    )(wanted, kv_blocks)


def attend(table_index, q_pairs, kv_local, kv_remote, first_block, per_source):
    sources, per = q_pairs.shape[:2]
    pairs = sources * per
    nlocal, nremote = kv_local.shape[0], kv_remote.shape[0]
    q_flat = q_pairs.reshape(pairs, BLK, LANES)

    def body(idx_ref, q_ref, loc_ref, rem_ref, o_ref, tab, s_buf, m_buf, sems):
        c0 = pltpu.make_async_copy(loc_ref, tab.at[pl.ds(0, nlocal)], sems.at[0])
        c1 = pltpu.make_async_copy(rem_ref, tab.at[pl.ds(nlocal, nremote)], sems.at[1])
        c0.start()
        c1.start()
        c0.wait()
        c1.wait()
        zeros = jnp.zeros((BLK, DH), jnp.bfloat16)

        def entry(pair, half):
            block = (pair // per) * per_source + first_block + 2 * (pair % per) + half
            return block * KPER

        def keys_of(base, jj):
            return jnp.concatenate(
                [tab[idx_ref[base + 2 * jj]], tab[idx_ref[base + 2 * jj + 1]]], axis=0
            )

        def score(pair, half):
            base = entry(pair, half)
            q = jnp.concatenate([q_ref[pair, :, half * DH : (half + 1) * DH], zeros], axis=1)
            top = None
            for jj in range(KPER // 2):
                s = lax.dot_general(q, keys_of(base, jj), NT, preferred_element_type=jnp.float32)
                s_buf[half, :, jj * 2 * BLK : (jj + 1) * 2 * BLK] = s
                both = jnp.maximum(s[:, :BLK], s[:, BLK:])
                top = both if top is None else jnp.maximum(top, both)
            m_buf[half] = jnp.broadcast_to(jnp.max(top, axis=1, keepdims=True), (BLK, LANES))

        def finish(pair, half):
            base = entry(pair, half)
            top = m_buf[half]
            top2 = jnp.concatenate([top, top], axis=1)
            total, acc = None, None
            for jj in range(KPER // 2):
                p = jnp.exp(s_buf[half, :, jj * 2 * BLK : (jj + 1) * 2 * BLK] - top2)
                both = p[:, :BLK] + p[:, BLK:]
                total = both if total is None else total + both
                part = lax.dot_general(
                    p.astype(jnp.bfloat16),
                    keys_of(base, jj),
                    NN,
                    preferred_element_type=jnp.float32,
                )
                acc = part if acc is None else acc + part
            total = jnp.sum(total, axis=1, keepdims=True)
            return (acc[:, DH:] / total).astype(jnp.bfloat16)

        score(0, 0)

        def step(i, carry):
            score(i, 1)
            a = finish(i, 0)
            score(jnp.minimum(i + 1, pairs - 1), 0)
            b = finish(i, 1)
            o_ref[i] = jnp.concatenate([a, b], axis=1)
            return carry

        lax.fori_loop(0, pairs, step, 0)

    out = pl.pallas_call(
        body,
        in_specs=[
            pl.BlockSpec(memory_space=pltpu.SMEM),
            pl.BlockSpec(memory_space=pltpu.VMEM),
            pl.BlockSpec(memory_space=pl.ANY),
            pl.BlockSpec(memory_space=pl.ANY),
        ],
        out_specs=pl.BlockSpec(memory_space=pltpu.VMEM),
        out_shape=jax.ShapeDtypeStruct((pairs, BLK, LANES), jnp.bfloat16),
        scratch_shapes=[
            pltpu.VMEM((nlocal + nremote, BLK, LANES), jnp.bfloat16),
            pltpu.VMEM((2, BLK, KPER * BLK), jnp.float32),
            pltpu.VMEM((2, BLK, LANES), jnp.float32),
            pltpu.SemaphoreType.DMA((2,)),
        ],
        compiler_params=pltpu.CompilerParams(vmem_limit_bytes=VMEM_LIMIT),
        cost_estimate=pl.CostEstimate(
            flops=pairs * 2 * KPER * BLK * BLK * LANES * 4,
            bytes_accessed=(nlocal + nremote + 2 * pairs) * BLK * LANES * 2,
            transcendentals=pairs * 2 * KPER * BLK * BLK,
        ),
        name="attend",
    )(table_index, q_flat, kv_local, kv_remote)
    return out.reshape(sources, per, BLK, LANES)


def unpack(o_pairs, tok, width, first_pair, into):
    heads, per = o_pairs.shape[:2]
    rows = per * 2 * BLK

    def body(o_ref, *rest):
        out_ref = rest[-1]
        for p in range(per):
            for c in range(heads // 2):
                cols = slice(c * LANES, (c + 1) * LANES)
                even, odd = o_ref[2 * c, p], o_ref[2 * c + 1, p]
                out_ref[2 * p * BLK : (2 * p + 1) * BLK, cols] = jnp.concatenate(
                    [even[:, :DH], odd[:, :DH]], axis=1
                )
                out_ref[(2 * p + 1) * BLK : (2 * p + 2) * BLK, cols] = jnp.concatenate(
                    [even[:, DH:], odd[:, DH:]], axis=1
                )

    row_block = first_pair // per
    in_specs = [pl.BlockSpec((heads, per, BLK, LANES), lambda i: (0, 0, 0, 0))]
    args = [o_pairs]
    if into is not None:
        in_specs.append(pl.BlockSpec(memory_space=pl.ANY))
        args.append(into)
    return pl.pallas_call(
        body,
        grid=(1,),
        in_specs=in_specs,
        out_specs=pl.BlockSpec((rows, width), lambda i: (row_block, 0)),
        out_shape=jax.ShapeDtypeStruct((tok, width), jnp.bfloat16),
        input_output_aliases={1: 0} if into is not None else {},
        cost_estimate=pl.CostEstimate(flops=0, bytes_accessed=4 * rows * width, transcendentals=0),
        name="unpack",
    )(*args)


def across(x, axis):
    return lax.all_to_all(x, axis, split_axis=0, concat_axis=0, tiled=True)


def on_device(chunks, query, key, value, pattern):
    tok, width = query.shape
    sources = lax.axis_size("head")
    ranges = lax.axis_size("ctx")
    own = lax.axis_index("ctx")
    per_source = tok // BLK
    count = sources * per_source

    per = per_source // (2 * chunks)
    q_send = [pack_q(query, per * c, per) for c in range(chunks)]
    q_first = across(q_send[0], "head")
    kv_send = pack_kv(key, value)

    rows = pattern[0]
    owner, pos = rows // count, rows % count
    of_range = owner[None] == jnp.arange(ranges, dtype=jnp.int32)[:, None, None]
    low = jnp.min(jnp.where(of_range, pos[None], count - 1), axis=(1, 2))
    high = jnp.max(jnp.where(of_range, pos[None], 0), axis=(1, 2))
    wanted = jnp.stack([low, high], axis=1)
    slot = jnp.sum(jnp.where(of_range, (pos[None] != low[:, None, None]).astype(jnp.int32), 0), axis=0)
    far = count + owner * PMOST + slot
    table_index = jnp.where(owner == own, pos, far).reshape(-1)

    asked = wanted[own ^ jnp.arange(ranges, dtype=jnp.int32)]
    bit = 1
    while bit < ranges:
        asked = asked.reshape(ranges // (2 * bit), 2, bit, PMOST)
        moved = lax.ppermute(asked[:, 1], "ctx", [(i, i ^ bit) for i in range(ranges)])
        asked = jnp.stack([asked[:, 0], moved], axis=1).reshape(ranges, PMOST)
        bit *= 2

    kv_send, asked, q_first = lax.optimization_barrier((kv_send, asked, q_first))
    kv_blocks = across(kv_send, "head").reshape(count, BLK, LANES)
    by_range = asked[own ^ jnp.arange(ranges, dtype=jnp.int32)]
    picked = pick_blocks(kv_blocks, by_range.reshape(-1))
    remote = across(picked.reshape(ranges, PMOST * BLK, LANES), "ctx")
    remote = remote.reshape(ranges * PMOST, BLK, LANES)

    out = None
    for c in range(chunks):
        if c == 0:
            q_pairs = q_first
        else:
            send, remote = lax.optimization_barrier((q_send[c], remote))
            q_pairs = across(send, "head")
        o_pairs = attend(table_index, q_pairs, kv_blocks, remote, 2 * per * c, per_source)
        o_pairs = across(o_pairs, "head")
        out = unpack(o_pairs, tok, width, per * c, out)
    return out


def solution(mesh):
    placed = (
        P(("ctx", "head"), None),
        P(("ctx", "head"), None),
        P(("ctx", "head"), None),
        P("head", "ctx", None),
    )
    return jax.shard_map(
        functools.partial(on_device, 2),
        mesh=mesh,
        in_specs=placed,
        out_specs=P(("ctx", "head"), None),
        check_vma=False,
    )
```

```python
import jax
import jax.numpy as jnp
from jax import lax
from jax.experimental import pallas as pl
from jax.experimental.pallas import tpu as pltpu
from jax.sharding import PartitionSpec as P

DH = 64
BLK = 128
KPER = 12
PMOST = 2
LANES = 2 * DH
NT = (((1,), (1,)), ((), ()))
NN = (((1,), (0,)), ((), ()))
VMEM_LIMIT = 48 * 1024 * 1024
WHOLE_VMEM = 63 * 1024 * 1024


def put_q(q_ref, o_ref, row, pairs):
    for p in range(pairs):
        for c in range(q_ref.shape[1] // LANES):
            cols = slice(c * LANES, (c + 1) * LANES)
            rows = slice(row + p * BLK, row + (p + 1) * BLK)
            a = q_ref[2 * p * BLK : (2 * p + 1) * BLK, cols] * jnp.bfloat16(0.125)
            b = q_ref[(2 * p + 1) * BLK : (2 * p + 2) * BLK, cols] * jnp.bfloat16(0.125)
            o_ref[2 * c, rows] = jnp.concatenate([a[:, :DH], b[:, :DH]], axis=1)
            o_ref[2 * c + 1, rows] = jnp.concatenate([a[:, DH:], b[:, DH:]], axis=1)


def pack_first(key, value, query, steps, kv_per, q_per):
    width = key.shape[1]
    kv_rows = kv_per * BLK
    rows = (kv_per + q_per) * BLK

    def body(k_ref, v_ref, q_ref, o_ref):
        for c in range(width // LANES):
            k = k_ref[:, c * LANES : (c + 1) * LANES]
            v = v_ref[:, c * LANES : (c + 1) * LANES]
            o_ref[2 * c, :kv_rows] = jnp.concatenate([k[:, :DH], v[:, :DH]], axis=1)
            o_ref[2 * c + 1, :kv_rows] = jnp.concatenate([k[:, DH:], v[:, DH:]], axis=1)
        put_q(q_ref, o_ref, kv_rows, q_per)

    kv_spec = pl.BlockSpec((kv_rows, width), lambda i: (i, 0))
    return pl.pallas_call(
        body,
        grid=(steps,),
        in_specs=[kv_spec, kv_spec, pl.BlockSpec((2 * q_per * BLK, width), lambda i: (i, 0))],
        out_specs=pl.BlockSpec((width // DH, rows, LANES), lambda i: (0, i, 0)),
        out_shape=jax.ShapeDtypeStruct((width // DH, steps * rows, LANES), jnp.bfloat16),
        compiler_params=pltpu.CompilerParams(vmem_limit_bytes=WHOLE_VMEM),
        cost_estimate=pl.CostEstimate(
            flops=0, bytes_accessed=4 * steps * rows * width, transcendentals=0
        ),
        name="pack_first",
    )(key, value, query)


def pack_rest(query, row_block, pairs):
    width = query.shape[1]
    shape = (width // DH, pairs * BLK, LANES)

    def body(q_ref, o_ref):
        put_q(q_ref, o_ref, 0, pairs)

    return pl.pallas_call(
        body,
        grid=(1,),
        in_specs=[pl.BlockSpec((2 * pairs * BLK, width), lambda i: (row_block, 0))],
        out_specs=pl.BlockSpec(shape, lambda i: (0, 0, 0)),
        out_shape=jax.ShapeDtypeStruct(shape, jnp.bfloat16),
        compiler_params=pltpu.CompilerParams(vmem_limit_bytes=WHOLE_VMEM),
        cost_estimate=pl.CostEstimate(
            flops=0, bytes_accessed=4 * pairs * BLK * width, transcendentals=0
        ),
        name="pack_rest",
    )(query)


def pick_blocks(kv_blocks, wanted):
    count = wanted.shape[0]

    def body(w_ref, kv_ref, o_ref, sem):
        copies = [
            pltpu.make_async_copy(kv_ref.at[w_ref[i]], o_ref.at[i], sem.at[i]) for i in range(count)
        ]
        for c in copies:
            c.start()
        for c in copies:
            c.wait()

    return pl.pallas_call(
        body,
        in_specs=[
            pl.BlockSpec(memory_space=pltpu.SMEM),
            pl.BlockSpec(memory_space=pl.ANY),
        ],
        out_specs=pl.BlockSpec(memory_space=pltpu.VMEM),
        out_shape=jax.ShapeDtypeStruct((count,) + kv_blocks.shape[1:], jnp.bfloat16),
        scratch_shapes=[pltpu.SemaphoreType.DMA((count,))],
        cost_estimate=pl.CostEstimate(
            flops=0, bytes_accessed=count * BLK * LANES * 4, transcendentals=0
        ),
        name="pick_blocks",
    )(wanted, kv_blocks)


def attend(table_index, q_pairs, tables, sources, per, first_block, per_source, q_place):
    pairs = sources * per
    starts = [0]
    for t in tables:
        starts.append(starts[-1] + t.shape[0])
    extra = [] if q_pairs is None else [q_pairs]

    def body(idx_ref, *refs):
        q_refs, refs = refs[: len(extra)], refs[len(extra) :]
        t_refs, (o_ref, tab, s_buf, m_buf, sems) = refs[: len(tables)], refs[len(tables) :]
        copies = [
            pltpu.make_async_copy(r, tab.at[pl.ds(starts[i], starts[i + 1] - starts[i])], sems.at[i])
            for i, r in enumerate(t_refs)
        ]
        for c in copies:
            c.start()
        for c in copies:
            c.wait()
        zeros = jnp.zeros((BLK, DH), jnp.bfloat16)

        def entry(pair, half):
            block = (pair // per) * per_source + first_block + 2 * (pair % per) + half
            return block * KPER

        def keys_of(base, jj):
            return jnp.concatenate(
                [tab[idx_ref[base + 2 * jj]], tab[idx_ref[base + 2 * jj + 1]]], axis=0
            )

        def score(pair, half):
            base = entry(pair, half)
            lanes = slice(half * DH, (half + 1) * DH)
            q = q_refs[0][pair, :, lanes] if extra else tab[q_place(pair), :, lanes]
            q = jnp.concatenate([q, zeros], axis=1)
            top = None
            for jj in range(KPER // 2):
                s = lax.dot_general(q, keys_of(base, jj), NT, preferred_element_type=jnp.float32)
                s_buf[half, :, jj * 2 * BLK : (jj + 1) * 2 * BLK] = s
                both = jnp.maximum(s[:, :BLK], s[:, BLK:])
                top = both if top is None else jnp.maximum(top, both)
            m_buf[half] = jnp.broadcast_to(jnp.max(top, axis=1, keepdims=True), (BLK, LANES))

        def finish(pair, half):
            base = entry(pair, half)
            top = m_buf[half]
            top2 = jnp.concatenate([top, top], axis=1)
            total, acc = None, None
            for jj in range(KPER // 2):
                p = jnp.exp(s_buf[half, :, jj * 2 * BLK : (jj + 1) * 2 * BLK] - top2)
                both = p[:, :BLK] + p[:, BLK:]
                total = both if total is None else total + both
                part = lax.dot_general(
                    p.astype(jnp.bfloat16),
                    keys_of(base, jj),
                    NN,
                    preferred_element_type=jnp.float32,
                )
                acc = part if acc is None else acc + part
            total = jnp.sum(total, axis=1, keepdims=True)
            return (acc[:, DH:] / total).astype(jnp.bfloat16)

        score(0, 0)

        def step(i, carry):
            score(i, 1)
            a = finish(i, 0)
            score(jnp.minimum(i + 1, pairs - 1), 0)
            b = finish(i, 1)
            o_ref[i] = jnp.concatenate([a, b], axis=1)
            return carry

        lax.fori_loop(0, pairs, step, 0)

    return pl.pallas_call(
        body,
        in_specs=[pl.BlockSpec(memory_space=pltpu.SMEM)]
        + [pl.BlockSpec(memory_space=pltpu.VMEM)] * len(extra)
        + [pl.BlockSpec(memory_space=pl.ANY)] * len(tables),
        out_specs=pl.BlockSpec(memory_space=pltpu.VMEM),
        out_shape=jax.ShapeDtypeStruct((pairs, BLK, LANES), jnp.bfloat16),
        scratch_shapes=[
            pltpu.VMEM((starts[-1], BLK, LANES), jnp.bfloat16),
            pltpu.VMEM((2, BLK, KPER * BLK), jnp.float32),
            pltpu.VMEM((2, BLK, LANES), jnp.float32),
            pltpu.SemaphoreType.DMA((len(tables),)),
        ],
        compiler_params=pltpu.CompilerParams(vmem_limit_bytes=VMEM_LIMIT),
        cost_estimate=pl.CostEstimate(
            flops=pairs * 2 * KPER * BLK * BLK * LANES * 4,
            bytes_accessed=(starts[-1] + 2 * pairs) * BLK * LANES * 2,
            transcendentals=pairs * 2 * KPER * BLK * BLK,
        ),
        name="attend",
    )(table_index, *extra, *tables)


def unpack(o_pairs, tok, width, first_pair, into):
    heads, per = o_pairs.shape[:2]
    rows = per * 2 * BLK

    def body(o_any, *rest):
        out_ref, o_ref, result, sem = rest[-4:]
        loads = [
            pltpu.make_async_copy(o_any.at[:, p], o_ref.at[:, p], sem.at[p]) for p in range(per)
        ]
        for load in loads:
            load.start()
        stores = []
        for p in range(per):
            loads[p].wait()
            for c in range(heads // 2):
                cols = slice(c * LANES, (c + 1) * LANES)
                even, odd = o_ref[2 * c, p], o_ref[2 * c + 1, p]
                result[2 * p * BLK : (2 * p + 1) * BLK, cols] = jnp.concatenate(
                    [even[:, :DH], odd[:, :DH]], axis=1
                )
                result[(2 * p + 1) * BLK : (2 * p + 2) * BLK, cols] = jnp.concatenate(
                    [even[:, DH:], odd[:, DH:]], axis=1
                )
            part = pl.ds(2 * p * BLK, 2 * BLK)
            start = 2 * (first_pair + p) * BLK
            stores.append(
                pltpu.make_async_copy(
                    result.at[part], out_ref.at[pl.ds(start, 2 * BLK)], sem.at[per + p]
                )
            )
            stores[-1].start()
        for store in stores:
            store.wait()

    in_specs = [pl.BlockSpec(memory_space=pl.ANY)]
    args = [o_pairs]
    if into is not None:
        in_specs.append(pl.BlockSpec(memory_space=pl.ANY))
        args.append(into)
    return pl.pallas_call(
        body,
        in_specs=in_specs,
        out_specs=pl.BlockSpec(memory_space=pl.ANY),
        out_shape=jax.ShapeDtypeStruct((tok, width), jnp.bfloat16),
        scratch_shapes=[
            pltpu.VMEM(o_pairs.shape, jnp.bfloat16),
            pltpu.VMEM((rows, width), jnp.bfloat16),
            pltpu.SemaphoreType.DMA((2 * per,)),
        ],
        input_output_aliases={1: 0} if into is not None else {},
        cost_estimate=pl.CostEstimate(flops=0, bytes_accessed=4 * rows * width, transcendentals=0),
        name="unpack",
    )(*args)


def across(x, axis):
    return lax.all_to_all(x, axis, split_axis=0, concat_axis=0, tiled=True)


def on_device(query, key, value, pattern):
    tok, width = query.shape
    sources = lax.axis_size("head")
    ranges = lax.axis_size("ctx")
    own = lax.axis_index("ctx")
    per_source = tok // BLK
    count = sources * per_source

    half = per_source // 2
    per = half // 2
    steps = per
    kv_per = per_source // steps
    stride = kv_per + 1

    rows = pattern[0]
    owner, pos = rows // count, rows % count
    of_range = owner[None] == jnp.arange(ranges, dtype=jnp.int32)[:, None, None]
    low = jnp.min(jnp.where(of_range, pos[None], count - 1), axis=(1, 2))
    high = jnp.max(jnp.where(of_range, pos[None], 0), axis=(1, 2))
    wanted = jnp.stack([low, high], axis=1)
    slot = jnp.sum(jnp.where(of_range, (pos[None] != low[:, None, None]).astype(jnp.int32), 0), axis=0)
    first_far = sources * steps * stride

    def place(p):
        return p // kv_per * stride + p % kv_per

    table_index = jnp.where(owner == own, place(pos), first_far + owner * PMOST + slot).reshape(-1)

    asked = across(wanted, "ctx")
    send = pack_first(key, value, query, steps, kv_per, 1)
    send, asked = lax.optimization_barrier((send, asked))
    first = across(send, "head").reshape(-1, BLK, LANES)
    send_rest = pack_rest(query, 1, per)
    picked = pick_blocks(first, place(asked).reshape(-1))
    remote = across(picked.reshape(ranges, PMOST * BLK, LANES), "ctx")
    send_rest, remote = lax.optimization_barrier((send_rest, remote))
    tables = [first, remote.reshape(-1, BLK, LANES)]
    q_rest = across(send_rest, "head").reshape(-1, BLK, LANES)

    out = None
    for c in range(2):
        o_pairs = attend(
            table_index,
            None if c == 0 else q_rest,
            tables,
            sources,
            per,
            half * c,
            per_source,
            lambda pair: pair * stride + kv_per,
        )
        o_pairs = across(o_pairs.reshape(sources, per, BLK, LANES), "head")
        out = unpack(o_pairs, tok, width, per * c, out)
    return out


def solution(mesh):
    placed = (
        P(("ctx", "head"), None),
        P(("ctx", "head"), None),
        P(("ctx", "head"), None),
        P("head", "ctx", None),
    )
    return jax.shard_map(
        on_device,
        mesh=mesh,
        in_specs=placed,
        out_specs=P(("ctx", "head"), None),
        check_vma=False,
    )
```

```python
import jax
import jax.numpy as jnp
from jax import lax
from jax.experimental import pallas as pl
from jax.experimental.pallas import tpu as pltpu
from jax.sharding import PartitionSpec as P

DH = 64
BLK = 128
KPER = 12
PMOST = 2
LANES = 2 * DH
NT = (((1,), (1,)), ((), ()))
NN = (((1,), (0,)), ((), ()))
ATTEND_VMEM = 12 * 1024 * 1024
SMALL_VMEM = 6 * 1024 * 1024
WHOLE_VMEM = 63 * 1024 * 1024


def put_q(q_ref, o_ref, row, pairs):
    for p in range(pairs):
        for c in range(q_ref.shape[1] // LANES):
            cols = slice(c * LANES, (c + 1) * LANES)
            rows = slice(row + p * BLK, row + (p + 1) * BLK)
            a = q_ref[2 * p * BLK : (2 * p + 1) * BLK, cols] * jnp.bfloat16(0.125)
            b = q_ref[(2 * p + 1) * BLK : (2 * p + 2) * BLK, cols] * jnp.bfloat16(0.125)
            o_ref[2 * c, rows] = jnp.concatenate([a[:, :DH], b[:, :DH]], axis=1)
            o_ref[2 * c + 1, rows] = jnp.concatenate([a[:, DH:], b[:, DH:]], axis=1)


def pack_first(key, value, query, steps, kv_per, q_per):
    width = key.shape[1]
    kv_rows = kv_per * BLK
    rows = (kv_per + q_per) * BLK

    def body(k_ref, v_ref, q_ref, o_ref):
        for c in range(width // LANES):
            k = k_ref[:, c * LANES : (c + 1) * LANES]
            v = v_ref[:, c * LANES : (c + 1) * LANES]
            o_ref[2 * c, :kv_rows] = jnp.concatenate([k[:, :DH], v[:, :DH]], axis=1)
            o_ref[2 * c + 1, :kv_rows] = jnp.concatenate([k[:, DH:], v[:, DH:]], axis=1)
        put_q(q_ref, o_ref, kv_rows, q_per)

    kv_spec = pl.BlockSpec((kv_rows, width), lambda i: (i, 0))
    return pl.pallas_call(
        body,
        grid=(steps,),
        in_specs=[kv_spec, kv_spec, pl.BlockSpec((2 * q_per * BLK, width), lambda i: (i, 0))],
        out_specs=pl.BlockSpec((width // DH, rows, LANES), lambda i: (0, i, 0)),
        out_shape=jax.ShapeDtypeStruct((width // DH, steps * rows, LANES), jnp.bfloat16),
        compiler_params=pltpu.CompilerParams(vmem_limit_bytes=WHOLE_VMEM),
        cost_estimate=pl.CostEstimate(
            flops=0, bytes_accessed=4 * steps * rows * width, transcendentals=0
        ),
        name="pack_first",
    )(key, value, query)


def pack_rest(query, row_block, pairs):
    width = query.shape[1]
    shape = (width // DH, pairs * BLK, LANES)

    def body(q_ref, o_ref):
        put_q(q_ref, o_ref, 0, pairs)

    return pl.pallas_call(
        body,
        grid=(1,),
        in_specs=[pl.BlockSpec((2 * pairs * BLK, width), lambda i: (row_block, 0))],
        out_specs=pl.BlockSpec(shape, lambda i: (0, 0, 0)),
        out_shape=jax.ShapeDtypeStruct(shape, jnp.bfloat16),
        compiler_params=pltpu.CompilerParams(vmem_limit_bytes=SMALL_VMEM),
        cost_estimate=pl.CostEstimate(
            flops=0, bytes_accessed=4 * pairs * BLK * width, transcendentals=0
        ),
        name="pack_rest",
    )(query)


def pick_blocks(kv_blocks, wanted):
    count = wanted.shape[0]

    def body(w_ref, kv_ref, o_ref, sem):
        copies = [
            pltpu.make_async_copy(kv_ref.at[w_ref[i]], o_ref.at[i], sem.at[i]) for i in range(count)
        ]
        for c in copies:
            c.start()
        for c in copies:
            c.wait()

    return pl.pallas_call(
        body,
        in_specs=[
            pl.BlockSpec(memory_space=pltpu.SMEM),
            pl.BlockSpec(memory_space=pl.ANY),
        ],
        out_specs=pl.BlockSpec(memory_space=pltpu.VMEM),
        out_shape=jax.ShapeDtypeStruct((count,) + kv_blocks.shape[1:], jnp.bfloat16),
        scratch_shapes=[pltpu.SemaphoreType.DMA((count,))],
        compiler_params=pltpu.CompilerParams(vmem_limit_bytes=SMALL_VMEM),
        cost_estimate=pl.CostEstimate(
            flops=0, bytes_accessed=count * BLK * LANES * 4, transcendentals=0
        ),
        name="pick_blocks",
    )(wanted, kv_blocks)


def take_queries(table, pairs):
    def body(t_ref, o_ref, sem):
        stride = t_ref.shape[0] // pairs
        copies = [
            pltpu.make_async_copy(t_ref.at[i * stride + stride - 1], o_ref.at[i], sem.at[i])
            for i in range(pairs)
        ]
        for c in copies:
            c.start()
        for c in copies:
            c.wait()

    return pl.pallas_call(
        body,
        in_specs=[pl.BlockSpec(memory_space=pl.ANY)],
        out_specs=pl.BlockSpec(memory_space=pltpu.VMEM),
        out_shape=jax.ShapeDtypeStruct((pairs, BLK, LANES), jnp.bfloat16),
        scratch_shapes=[pltpu.SemaphoreType.DMA((pairs,))],
        compiler_params=pltpu.CompilerParams(vmem_limit_bytes=SMALL_VMEM),
        cost_estimate=pl.CostEstimate(
            flops=0, bytes_accessed=pairs * BLK * LANES * 4, transcendentals=0
        ),
        name="take_queries",
    )(table)


def put_remote(table, remote, pairs):
    count = remote.shape[0]

    def body(t_ref, r_ref, o_ref, sem):
        stride = t_ref.shape[0] // pairs
        copies = [
            pltpu.make_async_copy(r_ref.at[i], o_ref.at[i * stride + stride - 1], sem.at[i])
            for i in range(count)
        ]
        for c in copies:
            c.start()
        for c in copies:
            c.wait()

    return pl.pallas_call(
        body,
        in_specs=[pl.BlockSpec(memory_space=pl.ANY)] * 2,
        out_specs=pl.BlockSpec(memory_space=pl.ANY),
        out_shape=jax.ShapeDtypeStruct(table.shape, jnp.bfloat16),
        scratch_shapes=[pltpu.SemaphoreType.DMA((count,))],
        input_output_aliases={0: 0},
        compiler_params=pltpu.CompilerParams(vmem_limit_bytes=SMALL_VMEM),
        cost_estimate=pl.CostEstimate(
            flops=0, bytes_accessed=count * BLK * LANES * 4, transcendentals=0
        ),
        name="put_remote",
    )(table, remote)


def attend(table_index, q_pairs, table, sources, per, first_block, per_source):
    pairs = sources * per

    def body(idx_ref, q_ref, tab, o_ref, s_buf, m_buf):
        zeros = jnp.zeros((BLK, DH), jnp.bfloat16)

        def entry(pair, half):
            block = (pair // per) * per_source + first_block + 2 * (pair % per) + half
            return block * KPER

        def keys_of(base, jj):
            return jnp.concatenate(
                [tab[idx_ref[base + 2 * jj]], tab[idx_ref[base + 2 * jj + 1]]], axis=0
            )

        def score(pair, half):
            base = entry(pair, half)
            lanes = slice(half * DH, (half + 1) * DH)
            q = jnp.concatenate([q_ref[pair, :, lanes], zeros], axis=1)
            top = None
            for jj in range(KPER // 2):
                s = lax.dot_general(q, keys_of(base, jj), NT, preferred_element_type=jnp.float32)
                s_buf[half, :, jj * 2 * BLK : (jj + 1) * 2 * BLK] = s
                both = jnp.maximum(s[:, :BLK], s[:, BLK:])
                top = both if top is None else jnp.maximum(top, both)
            m_buf[half] = jnp.broadcast_to(jnp.max(top, axis=1, keepdims=True), (BLK, LANES))

        def finish(pair, half):
            base = entry(pair, half)
            top = m_buf[half]
            top2 = jnp.concatenate([top, top], axis=1)
            total, acc = None, None
            for jj in range(KPER // 2):
                p = jnp.exp(s_buf[half, :, jj * 2 * BLK : (jj + 1) * 2 * BLK] - top2)
                both = p[:, :BLK] + p[:, BLK:]
                total = both if total is None else total + both
                part = lax.dot_general(
                    p.astype(jnp.bfloat16),
                    keys_of(base, jj),
                    NN,
                    preferred_element_type=jnp.float32,
                )
                acc = part if acc is None else acc + part
            total = jnp.sum(total, axis=1, keepdims=True)
            return (acc[:, DH:] / total).astype(jnp.bfloat16)

        score(0, 0)

        def step(i, carry):
            score(i, 1)
            a = finish(i, 0)
            score(jnp.minimum(i + 1, pairs - 1), 0)
            b = finish(i, 1)
            o_ref[i] = jnp.concatenate([a, b], axis=1)
            return carry

        lax.fori_loop(0, pairs, step, 0)

    return pl.pallas_call(
        body,
        in_specs=[
            pl.BlockSpec(memory_space=pltpu.SMEM),
            pl.BlockSpec(memory_space=pltpu.VMEM),
            pl.BlockSpec(memory_space=pltpu.VMEM),
        ],
        out_specs=pl.BlockSpec(memory_space=pltpu.VMEM),
        out_shape=jax.ShapeDtypeStruct((pairs, BLK, LANES), jnp.bfloat16),
        scratch_shapes=[
            pltpu.VMEM((2, BLK, KPER * BLK), jnp.float32),
            pltpu.VMEM((2, BLK, LANES), jnp.float32),
        ],
        compiler_params=pltpu.CompilerParams(vmem_limit_bytes=ATTEND_VMEM),
        cost_estimate=pl.CostEstimate(
            flops=pairs * 2 * KPER * BLK * BLK * LANES * 4,
            bytes_accessed=(table.shape[0] + 2 * pairs) * BLK * LANES * 2,
            transcendentals=pairs * 2 * KPER * BLK * BLK,
        ),
        name="attend",
    )(table_index, q_pairs, table)


def unpack(o_pairs, tok, width, first_pair, into):
    heads, per = o_pairs.shape[:2]
    rows = per * 2 * BLK

    def body(o_any, *rest):
        out_ref, o_ref, result, sem = rest[-4:]
        loads = [
            pltpu.make_async_copy(o_any.at[:, p], o_ref.at[:, p], sem.at[p]) for p in range(per)
        ]
        for load in loads:
            load.start()
        stores = []
        for p in range(per):
            loads[p].wait()
            for c in range(heads // 2):
                cols = slice(c * LANES, (c + 1) * LANES)
                even, odd = o_ref[2 * c, p], o_ref[2 * c + 1, p]
                result[2 * p * BLK : (2 * p + 1) * BLK, cols] = jnp.concatenate(
                    [even[:, :DH], odd[:, :DH]], axis=1
                )
                result[(2 * p + 1) * BLK : (2 * p + 2) * BLK, cols] = jnp.concatenate(
                    [even[:, DH:], odd[:, DH:]], axis=1
                )
            part = pl.ds(2 * p * BLK, 2 * BLK)
            start = 2 * (first_pair + p) * BLK
            stores.append(
                pltpu.make_async_copy(
                    result.at[part], out_ref.at[pl.ds(start, 2 * BLK)], sem.at[per + p]
                )
            )
            stores[-1].start()
        for store in stores:
            store.wait()

    in_specs = [pl.BlockSpec(memory_space=pl.ANY)]
    args = [o_pairs]
    if into is not None:
        in_specs.append(pl.BlockSpec(memory_space=pl.ANY))
        args.append(into)
    return pl.pallas_call(
        body,
        in_specs=in_specs,
        out_specs=pl.BlockSpec(memory_space=pl.ANY),
        out_shape=jax.ShapeDtypeStruct((tok, width), jnp.bfloat16),
        scratch_shapes=[
            pltpu.VMEM(o_pairs.shape, jnp.bfloat16),
            pltpu.VMEM((rows, width), jnp.bfloat16),
            pltpu.SemaphoreType.DMA((2 * per,)),
        ],
        input_output_aliases={1: 0} if into is not None else {},
        compiler_params=pltpu.CompilerParams(vmem_limit_bytes=SMALL_VMEM),
        cost_estimate=pl.CostEstimate(flops=0, bytes_accessed=4 * rows * width, transcendentals=0),
        name="unpack",
    )(*args)


def across(x, axis):
    return lax.all_to_all(x, axis, split_axis=0, concat_axis=0, tiled=True)


def on_device(query, key, value, pattern):
    tok, width = query.shape
    sources = lax.axis_size("head")
    ranges = lax.axis_size("ctx")
    own = lax.axis_index("ctx")
    per_source = tok // BLK
    count = sources * per_source

    half = per_source // 2
    per = half // 2
    steps = per
    kv_per = per_source // steps
    stride = kv_per + 1

    rows = pattern[0]
    owner, pos = rows // count, rows % count
    of_range = owner[None] == jnp.arange(ranges, dtype=jnp.int32)[:, None, None]
    low = jnp.min(jnp.where(of_range, pos[None], count - 1), axis=(1, 2))
    high = jnp.max(jnp.where(of_range, pos[None], 0), axis=(1, 2))
    wanted = jnp.stack([low, high], axis=1)
    slot = jnp.sum(jnp.where(of_range, (pos[None] != low[:, None, None]).astype(jnp.int32), 0), axis=0)

    def place(p):
        return p // kv_per * stride + p % kv_per

    far = (owner * PMOST + slot) * stride + kv_per
    table_index = jnp.where(owner == own, place(pos), far).reshape(-1)

    asked = across(wanted, "ctx")
    send = pack_first(key, value, query, steps, kv_per, 1)
    send, asked = lax.optimization_barrier((send, asked))
    first = across(send, "head").reshape(-1, BLK, LANES)
    send_rest = pack_rest(query, 1, per)
    picked = pick_blocks(first, place(asked).reshape(-1))
    remote = across(picked.reshape(ranges, PMOST * BLK, LANES), "ctx")
    q_first = take_queries(first, sources * per)
    send_rest, remote, q_first = lax.optimization_barrier((send_rest, remote, q_first))
    table = put_remote(first, remote.reshape(-1, BLK, LANES), sources * per)
    q_rest = across(send_rest, "head").reshape(-1, BLK, LANES)

    out = None
    for c, q_pairs in enumerate((q_first, q_rest)):
        o_pairs = attend(table_index, q_pairs, table, sources, per, half * c, per_source)
        o_pairs = across(o_pairs.reshape(sources, per, BLK, LANES), "head")
        out = unpack(o_pairs, tok, width, per * c, out)
    return out


def solution(mesh):
    placed = (
        P(("ctx", "head"), None),
        P(("ctx", "head"), None),
        P(("ctx", "head"), None),
        P("head", "ctx", None),
    )
    return jax.shard_map(
        on_device,
        mesh=mesh,
        in_specs=placed,
        out_specs=P(("ctx", "head"), None),
        check_vma=False,
    )
```

```python
import jax
import jax.numpy as jnp
from jax import lax
from jax.experimental import pallas as pl
from jax.experimental.pallas import tpu as pltpu
from jax.sharding import PartitionSpec as P

DH = 64
BLK = 128
KPER = 12
PMOST = 2
LANES = 2 * DH
NT = (((1,), (1,)), ((), ()))
NN = (((1,), (0,)), ((), ()))
ATTEND_VMEM = 12 * 1024 * 1024
SMALL_VMEM = 6 * 1024 * 1024
WHOLE_VMEM = 63 * 1024 * 1024


def put_q(q_ref, o_ref, row, pairs):
    for p in range(pairs):
        for c in range(q_ref.shape[1] // LANES):
            cols = slice(c * LANES, (c + 1) * LANES)
            rows = slice(row + p * BLK, row + (p + 1) * BLK)
            a = q_ref[2 * p * BLK : (2 * p + 1) * BLK, cols] * jnp.bfloat16(0.125)
            b = q_ref[(2 * p + 1) * BLK : (2 * p + 2) * BLK, cols] * jnp.bfloat16(0.125)
            o_ref[2 * c, rows] = jnp.concatenate([a[:, :DH], b[:, :DH]], axis=1)
            o_ref[2 * c + 1, rows] = jnp.concatenate([a[:, DH:], b[:, DH:]], axis=1)


def pack_first(key, value, query, steps, kv_per, q_per):
    width = key.shape[1]
    kv_rows = kv_per * BLK
    rows = (kv_per + q_per) * BLK

    def body(k_ref, v_ref, q_ref, o_ref):
        for c in range(width // LANES):
            k = k_ref[:, c * LANES : (c + 1) * LANES]
            v = v_ref[:, c * LANES : (c + 1) * LANES]
            o_ref[2 * c, :kv_rows] = jnp.concatenate([k[:, :DH], v[:, :DH]], axis=1)
            o_ref[2 * c + 1, :kv_rows] = jnp.concatenate([k[:, DH:], v[:, DH:]], axis=1)
        put_q(q_ref, o_ref, kv_rows, q_per)

    kv_spec = pl.BlockSpec((kv_rows, width), lambda i: (i, 0))
    return pl.pallas_call(
        body,
        grid=(steps,),
        in_specs=[kv_spec, kv_spec, pl.BlockSpec((2 * q_per * BLK, width), lambda i: (i, 0))],
        out_specs=pl.BlockSpec((width // DH, rows, LANES), lambda i: (0, i, 0)),
        out_shape=jax.ShapeDtypeStruct((width // DH, steps * rows, LANES), jnp.bfloat16),
        compiler_params=pltpu.CompilerParams(vmem_limit_bytes=WHOLE_VMEM),
        cost_estimate=pl.CostEstimate(
            flops=0, bytes_accessed=4 * steps * rows * width, transcendentals=0
        ),
        name="pack_first",
    )(key, value, query)


def pack_rest(query, row_block, pairs):
    width = query.shape[1]
    shape = (width // DH, pairs * BLK, LANES)

    def body(q_ref, o_ref):
        put_q(q_ref, o_ref, 0, pairs)

    return pl.pallas_call(
        body,
        grid=(1,),
        in_specs=[pl.BlockSpec((2 * pairs * BLK, width), lambda i: (row_block, 0))],
        out_specs=pl.BlockSpec(shape, lambda i: (0, 0, 0)),
        out_shape=jax.ShapeDtypeStruct(shape, jnp.bfloat16),
        compiler_params=pltpu.CompilerParams(vmem_limit_bytes=SMALL_VMEM),
        cost_estimate=pl.CostEstimate(
            flops=0, bytes_accessed=4 * pairs * BLK * width, transcendentals=0
        ),
        name="pack_rest",
    )(query)


def pick_blocks(kv_blocks, wanted):
    count = wanted.shape[0]

    def body(w_ref, kv_ref, o_ref, sem):
        copies = [
            pltpu.make_async_copy(kv_ref.at[w_ref[i]], o_ref.at[i], sem.at[i]) for i in range(count)
        ]
        for c in copies:
            c.start()
        for c in copies:
            c.wait()

    return pl.pallas_call(
        body,
        in_specs=[
            pl.BlockSpec(memory_space=pltpu.SMEM),
            pl.BlockSpec(memory_space=pl.ANY),
        ],
        out_specs=pl.BlockSpec(memory_space=pltpu.VMEM),
        out_shape=jax.ShapeDtypeStruct((count,) + kv_blocks.shape[1:], jnp.bfloat16),
        scratch_shapes=[pltpu.SemaphoreType.DMA((count,))],
        compiler_params=pltpu.CompilerParams(vmem_limit_bytes=SMALL_VMEM),
        cost_estimate=pl.CostEstimate(
            flops=0, bytes_accessed=count * BLK * LANES * 4, transcendentals=0
        ),
        name="pick_blocks",
    )(wanted, kv_blocks)


def take_queries(table, pairs):
    def body(t_ref, o_ref, sem):
        stride = t_ref.shape[0] // pairs
        copies = [
            pltpu.make_async_copy(t_ref.at[i * stride + stride - 1], o_ref.at[i], sem.at[i])
            for i in range(pairs)
        ]
        for c in copies:
            c.start()
        for c in copies:
            c.wait()

    return pl.pallas_call(
        body,
        in_specs=[pl.BlockSpec(memory_space=pl.ANY)],
        out_specs=pl.BlockSpec(memory_space=pltpu.VMEM),
        out_shape=jax.ShapeDtypeStruct((pairs, BLK, LANES), jnp.bfloat16),
        scratch_shapes=[pltpu.SemaphoreType.DMA((pairs,))],
        compiler_params=pltpu.CompilerParams(vmem_limit_bytes=SMALL_VMEM),
        cost_estimate=pl.CostEstimate(
            flops=0, bytes_accessed=pairs * BLK * LANES * 4, transcendentals=0
        ),
        name="take_queries",
    )(table)


def put_remote(table, remote, pairs):
    count = remote.shape[0]

    def body(t_ref, r_ref, o_ref, sem):
        stride = t_ref.shape[0] // pairs
        copies = [
            pltpu.make_async_copy(r_ref.at[i], o_ref.at[i * stride + stride - 1], sem.at[i])
            for i in range(count)
        ]
        for c in copies:
            c.start()
        for c in copies:
            c.wait()

    return pl.pallas_call(
        body,
        in_specs=[pl.BlockSpec(memory_space=pl.ANY)] * 2,
        out_specs=pl.BlockSpec(memory_space=pl.ANY),
        out_shape=jax.ShapeDtypeStruct(table.shape, jnp.bfloat16),
        scratch_shapes=[pltpu.SemaphoreType.DMA((count,))],
        input_output_aliases={0: 0},
        compiler_params=pltpu.CompilerParams(vmem_limit_bytes=SMALL_VMEM),
        cost_estimate=pl.CostEstimate(
            flops=0, bytes_accessed=count * BLK * LANES * 4, transcendentals=0
        ),
        name="put_remote",
    )(table, remote)


def attend(table_index, q_pairs, table, sources, per, first_block, per_source):
    pairs = sources * per

    def body(idx_ref, q_ref, tab, o_ref, s_buf, m_buf):
        zeros = jnp.zeros((BLK, DH), jnp.bfloat16)

        def entry(pair, half):
            block = (pair // per) * per_source + first_block + 2 * (pair % per) + half
            return block * KPER

        def keys_of(base, jj):
            return jnp.concatenate(
                [tab[idx_ref[base + 2 * jj]], tab[idx_ref[base + 2 * jj + 1]]], axis=0
            )

        def score(pair, half):
            base = entry(pair, half)
            lanes = slice(half * DH, (half + 1) * DH)
            q = jnp.concatenate([q_ref[pair, :, lanes], zeros], axis=1)
            top = None
            for jj in range(KPER // 2):
                s = lax.dot_general(q, keys_of(base, jj), NT, preferred_element_type=jnp.float32)
                s_buf[half, :, jj * 2 * BLK : (jj + 1) * 2 * BLK] = s
                both = jnp.maximum(s[:, :BLK], s[:, BLK:])
                top = both if top is None else jnp.maximum(top, both)
            m_buf[half] = jnp.broadcast_to(jnp.max(top, axis=1, keepdims=True), (BLK, LANES))

        def finish(pair, half):
            base = entry(pair, half)
            top = m_buf[half]
            top2 = jnp.concatenate([top, top], axis=1)
            total, acc = None, None
            for jj in range(KPER // 2):
                p = jnp.exp(s_buf[half, :, jj * 2 * BLK : (jj + 1) * 2 * BLK] - top2)
                both = p[:, :BLK] + p[:, BLK:]
                total = both if total is None else total + both
                part = lax.dot_general(
                    p.astype(jnp.bfloat16),
                    keys_of(base, jj),
                    NN,
                    preferred_element_type=jnp.float32,
                )
                acc = part if acc is None else acc + part
            total = jnp.sum(total, axis=1, keepdims=True)
            return (acc[:, DH:] / total).astype(jnp.bfloat16)

        score(0, 0)

        def step(i, carry):
            score(i, 1)
            a = finish(i, 0)
            score(jnp.minimum(i + 1, pairs - 1), 0)
            b = finish(i, 1)
            o_ref[i] = jnp.concatenate([a, b], axis=1)
            return carry

        lax.fori_loop(0, pairs, step, 0, unroll=8)

    return pl.pallas_call(
        body,
        in_specs=[
            pl.BlockSpec(memory_space=pltpu.SMEM),
            pl.BlockSpec(memory_space=pltpu.VMEM),
            pl.BlockSpec(memory_space=pltpu.VMEM),
        ],
        out_specs=pl.BlockSpec(memory_space=pltpu.VMEM),
        out_shape=jax.ShapeDtypeStruct((pairs, BLK, LANES), jnp.bfloat16),
        scratch_shapes=[
            pltpu.VMEM((2, BLK, KPER * BLK), jnp.float32),
            pltpu.VMEM((2, BLK, LANES), jnp.float32),
        ],
        compiler_params=pltpu.CompilerParams(vmem_limit_bytes=ATTEND_VMEM),
        cost_estimate=pl.CostEstimate(
            flops=pairs * 2 * KPER * BLK * BLK * LANES * 4,
            bytes_accessed=(table.shape[0] + 2 * pairs) * BLK * LANES * 2,
            transcendentals=pairs * 2 * KPER * BLK * BLK,
        ),
        name="attend",
    )(table_index, q_pairs, table)


def unpack(o_pairs, tok, width, first_pair, into):
    heads, per = o_pairs.shape[:2]
    rows = per * 2 * BLK

    def body(o_any, *rest):
        out_ref, o_ref, result, sem = rest[-4:]
        loads = [
            pltpu.make_async_copy(o_any.at[:, p], o_ref.at[:, p], sem.at[p]) for p in range(per)
        ]
        for load in loads:
            load.start()
        stores = []
        for p in range(per):
            loads[p].wait()
            for c in range(heads // 2):
                cols = slice(c * LANES, (c + 1) * LANES)
                even, odd = o_ref[2 * c, p], o_ref[2 * c + 1, p]
                result[2 * p * BLK : (2 * p + 1) * BLK, cols] = jnp.concatenate(
                    [even[:, :DH], odd[:, :DH]], axis=1
                )
                result[(2 * p + 1) * BLK : (2 * p + 2) * BLK, cols] = jnp.concatenate(
                    [even[:, DH:], odd[:, DH:]], axis=1
                )
            part = pl.ds(2 * p * BLK, 2 * BLK)
            start = 2 * (first_pair + p) * BLK
            stores.append(
                pltpu.make_async_copy(
                    result.at[part], out_ref.at[pl.ds(start, 2 * BLK)], sem.at[per + p]
                )
            )
            stores[-1].start()
        for store in stores:
            store.wait()

    in_specs = [pl.BlockSpec(memory_space=pl.ANY)]
    args = [o_pairs]
    if into is not None:
        in_specs.append(pl.BlockSpec(memory_space=pl.ANY))
        args.append(into)
    return pl.pallas_call(
        body,
        in_specs=in_specs,
        out_specs=pl.BlockSpec(memory_space=pl.ANY),
        out_shape=jax.ShapeDtypeStruct((tok, width), jnp.bfloat16),
        scratch_shapes=[
            pltpu.VMEM(o_pairs.shape, jnp.bfloat16),
            pltpu.VMEM((rows, width), jnp.bfloat16),
            pltpu.SemaphoreType.DMA((2 * per,)),
        ],
        input_output_aliases={1: 0} if into is not None else {},
        compiler_params=pltpu.CompilerParams(vmem_limit_bytes=SMALL_VMEM),
        cost_estimate=pl.CostEstimate(flops=0, bytes_accessed=4 * rows * width, transcendentals=0),
        name="unpack",
    )(*args)


def across(x, axis):
    return lax.all_to_all(x, axis, split_axis=0, concat_axis=0, tiled=True)


def on_device(query, key, value, pattern):
    tok, width = query.shape
    sources = lax.axis_size("head")
    ranges = lax.axis_size("ctx")
    own = lax.axis_index("ctx")
    per_source = tok // BLK
    count = sources * per_source

    half = per_source // 2
    per = half // 2
    steps = per
    kv_per = per_source // steps
    stride = kv_per + 1

    rows = pattern[0]
    owner, pos = rows // count, rows % count
    of_range = owner[None] == jnp.arange(ranges, dtype=jnp.int32)[:, None, None]
    low = jnp.min(jnp.where(of_range, pos[None], count - 1), axis=(1, 2))
    high = jnp.max(jnp.where(of_range, pos[None], 0), axis=(1, 2))
    wanted = jnp.stack([low, high], axis=1)
    slot = jnp.sum(jnp.where(of_range, (pos[None] != low[:, None, None]).astype(jnp.int32), 0), axis=0)

    def place(p):
        return p // kv_per * stride + p % kv_per

    far = (owner * PMOST + slot) * stride + kv_per
    table_index = jnp.where(owner == own, place(pos), far).reshape(-1)

    asked = across(wanted, "ctx")
    send = pack_first(key, value, query, steps, kv_per, 1)
    send, asked = lax.optimization_barrier((send, asked))
    first = across(send, "head").reshape(-1, BLK, LANES)
    send_rest = pack_rest(query, 1, per)
    picked = pick_blocks(first, place(asked).reshape(-1))
    remote = across(picked.reshape(ranges, PMOST * BLK, LANES), "ctx")
    q_first = take_queries(first, sources * per)
    send_rest, remote, q_first = lax.optimization_barrier((send_rest, remote, q_first))
    table = put_remote(first, remote.reshape(-1, BLK, LANES), sources * per)
    q_rest = across(send_rest, "head").reshape(-1, BLK, LANES)

    out = None
    for c, q_pairs in enumerate((q_first, q_rest)):
        o_pairs = attend(table_index, q_pairs, table, sources, per, half * c, per_source)
        o_pairs = across(o_pairs.reshape(sources, per, BLK, LANES), "head")
        out = unpack(o_pairs, tok, width, per * c, out)
    return out


def solution(mesh):
    placed = (
        P(("ctx", "head"), None),
        P(("ctx", "head"), None),
        P(("ctx", "head"), None),
        P("head", "ctx", None),
    )
    return jax.shard_map(
        on_device,
        mesh=mesh,
        in_specs=placed,
        out_specs=P(("ctx", "head"), None),
        check_vma=False,
    )
```

```python
import jax
import jax.numpy as jnp
from jax import lax
from jax.experimental import pallas as pl
from jax.experimental.pallas import tpu as pltpu
from jax.sharding import PartitionSpec as P

DH = 64
BLK = 128
KPER = 12
PMOST = 2
LANES = 2 * DH
NT = (((1,), (1,)), ((), ()))
NN = (((1,), (0,)), ((), ()))
ATTEND_VMEM = 12 * 1024 * 1024
SMALL_VMEM = 6 * 1024 * 1024
WHOLE_VMEM = 63 * 1024 * 1024


def put_q(q_ref, o_ref, row, pairs):
    for p in range(pairs):
        for c in range(q_ref.shape[1] // LANES):
            cols = slice(c * LANES, (c + 1) * LANES)
            rows = slice(row + p * BLK, row + (p + 1) * BLK)
            a = q_ref[2 * p * BLK : (2 * p + 1) * BLK, cols] * jnp.bfloat16(0.125)
            b = q_ref[(2 * p + 1) * BLK : (2 * p + 2) * BLK, cols] * jnp.bfloat16(0.125)
            o_ref[2 * c, rows] = jnp.concatenate([a[:, :DH], b[:, :DH]], axis=1)
            o_ref[2 * c + 1, rows] = jnp.concatenate([a[:, DH:], b[:, DH:]], axis=1)


def pack_first(key, value, query, steps, kv_per, q_per):
    width = key.shape[1]
    kv_rows = kv_per * BLK
    rows = (kv_per + q_per) * BLK

    def body(k_ref, v_ref, q_ref, o_ref):
        for c in range(width // LANES):
            k = k_ref[:, c * LANES : (c + 1) * LANES]
            v = v_ref[:, c * LANES : (c + 1) * LANES]
            o_ref[2 * c, :kv_rows] = jnp.concatenate([k[:, :DH], v[:, :DH]], axis=1)
            o_ref[2 * c + 1, :kv_rows] = jnp.concatenate([k[:, DH:], v[:, DH:]], axis=1)
        put_q(q_ref, o_ref, kv_rows, q_per)

    kv_spec = pl.BlockSpec((kv_rows, width), lambda i: (i, 0))
    return pl.pallas_call(
        body,
        grid=(steps,),
        in_specs=[kv_spec, kv_spec, pl.BlockSpec((2 * q_per * BLK, width), lambda i: (i, 0))],
        out_specs=pl.BlockSpec((width // DH, rows, LANES), lambda i: (0, i, 0)),
        out_shape=jax.ShapeDtypeStruct((width // DH, steps * rows, LANES), jnp.bfloat16),
        compiler_params=pltpu.CompilerParams(vmem_limit_bytes=WHOLE_VMEM),
        cost_estimate=pl.CostEstimate(
            flops=0, bytes_accessed=4 * steps * rows * width, transcendentals=0
        ),
        name="pack_first",
    )(key, value, query)


def pack_rest(query, row_block, pairs):
    width = query.shape[1]
    shape = (width // DH, pairs * BLK, LANES)

    def body(q_ref, o_ref):
        put_q(q_ref, o_ref, 0, pairs)

    return pl.pallas_call(
        body,
        grid=(1,),
        in_specs=[pl.BlockSpec((2 * pairs * BLK, width), lambda i: (row_block, 0))],
        out_specs=pl.BlockSpec(shape, lambda i: (0, 0, 0)),
        out_shape=jax.ShapeDtypeStruct(shape, jnp.bfloat16),
        compiler_params=pltpu.CompilerParams(vmem_limit_bytes=SMALL_VMEM),
        cost_estimate=pl.CostEstimate(
            flops=0, bytes_accessed=4 * pairs * BLK * width, transcendentals=0
        ),
        name="pack_rest",
    )(query)


def pick_blocks(kv_blocks, wanted):
    count = wanted.shape[0]

    def body(w_ref, kv_ref, o_ref, sem):
        copies = [
            pltpu.make_async_copy(kv_ref.at[w_ref[i]], o_ref.at[i], sem.at[i]) for i in range(count)
        ]
        for c in copies:
            c.start()
        for c in copies:
            c.wait()

    return pl.pallas_call(
        body,
        in_specs=[
            pl.BlockSpec(memory_space=pltpu.SMEM),
            pl.BlockSpec(memory_space=pl.ANY),
        ],
        out_specs=pl.BlockSpec(memory_space=pltpu.VMEM),
        out_shape=jax.ShapeDtypeStruct((count,) + kv_blocks.shape[1:], jnp.bfloat16),
        scratch_shapes=[pltpu.SemaphoreType.DMA((count,))],
        compiler_params=pltpu.CompilerParams(vmem_limit_bytes=SMALL_VMEM),
        cost_estimate=pl.CostEstimate(
            flops=0, bytes_accessed=count * BLK * LANES * 4, transcendentals=0
        ),
        name="pick_blocks",
    )(wanted, kv_blocks)


def take_queries(table, pairs):
    def body(t_ref, o_ref, sem):
        stride = t_ref.shape[0] // pairs
        copies = [
            pltpu.make_async_copy(t_ref.at[i * stride + stride - 1], o_ref.at[i], sem.at[i])
            for i in range(pairs)
        ]
        for c in copies:
            c.start()
        for c in copies:
            c.wait()

    return pl.pallas_call(
        body,
        in_specs=[pl.BlockSpec(memory_space=pl.ANY)],
        out_specs=pl.BlockSpec(memory_space=pltpu.VMEM),
        out_shape=jax.ShapeDtypeStruct((pairs, BLK, LANES), jnp.bfloat16),
        scratch_shapes=[pltpu.SemaphoreType.DMA((pairs,))],
        compiler_params=pltpu.CompilerParams(vmem_limit_bytes=SMALL_VMEM),
        cost_estimate=pl.CostEstimate(
            flops=0, bytes_accessed=pairs * BLK * LANES * 4, transcendentals=0
        ),
        name="take_queries",
    )(table)


def put_remote(table, remote, pairs):
    count = remote.shape[0]

    def body(t_ref, r_ref, o_ref, sem):
        stride = t_ref.shape[0] // pairs
        copies = [
            pltpu.make_async_copy(r_ref.at[i], o_ref.at[i * stride + stride - 1], sem.at[i])
            for i in range(count)
        ]
        for c in copies:
            c.start()
        for c in copies:
            c.wait()

    return pl.pallas_call(
        body,
        in_specs=[pl.BlockSpec(memory_space=pl.ANY)] * 2,
        out_specs=pl.BlockSpec(memory_space=pl.ANY),
        out_shape=jax.ShapeDtypeStruct(table.shape, jnp.bfloat16),
        scratch_shapes=[pltpu.SemaphoreType.DMA((count,))],
        input_output_aliases={0: 0},
        compiler_params=pltpu.CompilerParams(vmem_limit_bytes=SMALL_VMEM),
        cost_estimate=pl.CostEstimate(
            flops=0, bytes_accessed=count * BLK * LANES * 4, transcendentals=0
        ),
        name="put_remote",
    )(table, remote)


def attend(table_index, q_pairs, table, sources, per, first_block, per_source):
    pairs = sources * per

    def body(idx_ref, q_ref, tab, o_ref, s_buf, m_buf):
        zeros = jnp.zeros((BLK, DH), jnp.bfloat16)

        def entry(pair, half):
            block = (pair // per) * per_source + first_block + 2 * (pair % per) + half
            return block * KPER

        def keys_of(base, jj):
            return jnp.concatenate(
                [tab[idx_ref[base + 2 * jj]], tab[idx_ref[base + 2 * jj + 1]]], axis=0
            )

        def score(pair, half):
            base = entry(pair, half)
            lanes = slice(half * DH, (half + 1) * DH)
            q = jnp.concatenate([q_ref[pair, :, lanes], zeros], axis=1)
            top = None
            for jj in range(KPER // 2):
                s = lax.dot_general(q, keys_of(base, jj), NT, preferred_element_type=jnp.float32)
                s_buf[half, :, jj * 2 * BLK : (jj + 1) * 2 * BLK] = s
                both = jnp.maximum(s[:, :BLK], s[:, BLK:])
                top = both if top is None else jnp.maximum(top, both)
            m_buf[half] = jnp.broadcast_to(jnp.max(top, axis=1, keepdims=True), (BLK, LANES))

        def finish(pair, half):
            base = entry(pair, half)
            top = m_buf[half]
            top2 = jnp.concatenate([top, top], axis=1)
            total, acc = None, None
            for jj in range(KPER // 2):
                p = jnp.exp(s_buf[half, :, jj * 2 * BLK : (jj + 1) * 2 * BLK] - top2)
                both = p[:, :BLK] + p[:, BLK:]
                total = both if total is None else total + both
                part = lax.dot_general(
                    p.astype(jnp.bfloat16),
                    keys_of(base, jj),
                    NN,
                    preferred_element_type=jnp.float32,
                )
                acc = part if acc is None else acc + part
            total = jnp.sum(total, axis=1, keepdims=True)
            return (acc[:, DH:] / total).astype(jnp.bfloat16)

        score(0, 0)

        def step(i, carry):
            score(i, 1)
            a = finish(i, 0)
            score(jnp.minimum(i + 1, pairs - 1), 0)
            b = finish(i, 1)
            o_ref[i] = jnp.concatenate([a, b], axis=1)
            return carry

        lax.fori_loop(0, pairs, step, 0, unroll=8)

    return pl.pallas_call(
        body,
        in_specs=[
            pl.BlockSpec(memory_space=pltpu.SMEM),
            pl.BlockSpec(memory_space=pltpu.VMEM),
            pl.BlockSpec(memory_space=pltpu.VMEM),
        ],
        out_specs=pl.BlockSpec(memory_space=pltpu.VMEM),
        out_shape=jax.ShapeDtypeStruct((pairs, BLK, LANES), jnp.bfloat16),
        scratch_shapes=[
            pltpu.VMEM((2, BLK, KPER * BLK), jnp.float32),
            pltpu.VMEM((2, BLK, LANES), jnp.float32),
        ],
        compiler_params=pltpu.CompilerParams(vmem_limit_bytes=ATTEND_VMEM),
        cost_estimate=pl.CostEstimate(
            flops=pairs * 2 * KPER * BLK * BLK * LANES * 4,
            bytes_accessed=(table.shape[0] + 2 * pairs) * BLK * LANES * 2,
            transcendentals=pairs * 2 * KPER * BLK * BLK,
        ),
        name="attend",
    )(table_index, q_pairs, table)


def unpack(o_pairs, tok, width, first_pair, into):
    heads, per = o_pairs.shape[:2]
    rows = per * 2 * BLK

    def body(o_any, *rest):
        out_ref, o_ref, result, sem = rest[-4:]
        loads = [
            pltpu.make_async_copy(o_any.at[:, p], o_ref.at[:, p], sem.at[p]) for p in range(per)
        ]
        for load in loads:
            load.start()
        stores = []
        for p in range(per):
            loads[p].wait()
            for c in range(heads // 2):
                cols = slice(c * LANES, (c + 1) * LANES)
                even, odd = o_ref[2 * c, p], o_ref[2 * c + 1, p]
                result[2 * p * BLK : (2 * p + 1) * BLK, cols] = jnp.concatenate(
                    [even[:, :DH], odd[:, :DH]], axis=1
                )
                result[(2 * p + 1) * BLK : (2 * p + 2) * BLK, cols] = jnp.concatenate(
                    [even[:, DH:], odd[:, DH:]], axis=1
                )
            part = pl.ds(2 * p * BLK, 2 * BLK)
            start = 2 * (first_pair + p) * BLK
            stores.append(
                pltpu.make_async_copy(
                    result.at[part], out_ref.at[pl.ds(start, 2 * BLK)], sem.at[per + p]
                )
            )
            stores[-1].start()
        for store in stores:
            store.wait()

    in_specs = [pl.BlockSpec(memory_space=pl.ANY)]
    args = [o_pairs]
    if into is not None:
        in_specs.append(pl.BlockSpec(memory_space=pl.ANY))
        args.append(into)
    return pl.pallas_call(
        body,
        in_specs=in_specs,
        out_specs=pl.BlockSpec(memory_space=pl.ANY),
        out_shape=jax.ShapeDtypeStruct((tok, width), jnp.bfloat16),
        scratch_shapes=[
            pltpu.VMEM(o_pairs.shape, jnp.bfloat16),
            pltpu.VMEM((rows, width), jnp.bfloat16),
            pltpu.SemaphoreType.DMA((2 * per,)),
        ],
        input_output_aliases={1: 0} if into is not None else {},
        compiler_params=pltpu.CompilerParams(vmem_limit_bytes=SMALL_VMEM),
        cost_estimate=pl.CostEstimate(flops=0, bytes_accessed=4 * rows * width, transcendentals=0),
        name="unpack",
    )(*args)


def across(x, axis):
    return lax.all_to_all(x, axis, split_axis=0, concat_axis=0, tiled=True)


def on_device(query, key, value, pattern):
    tok, width = query.shape
    sources = lax.axis_size("head")
    ranges = lax.axis_size("ctx")
    own = lax.axis_index("ctx")
    per_source = tok // BLK
    count = sources * per_source

    half = per_source // 2
    per = half // 2
    steps = per
    kv_per = per_source // steps
    stride = kv_per + 1

    rows = pattern[0]
    owner, pos = rows // count, rows % count
    of_range = owner[None] == jnp.arange(ranges, dtype=jnp.int32)[:, None, None]
    low = jnp.min(jnp.where(of_range, pos[None], count - 1), axis=(1, 2))
    high = jnp.max(jnp.where(of_range, pos[None], 0), axis=(1, 2))
    wanted = jnp.stack([low, high], axis=1)
    slot = jnp.sum(jnp.where(of_range, (pos[None] != low[:, None, None]).astype(jnp.int32), 0), axis=0)

    def place(p):
        return p // kv_per * stride + p % kv_per

    far = (owner * PMOST + slot) * stride + kv_per
    table_index = jnp.where(owner == own, place(pos), far).reshape(-1)

    asked = wanted[own ^ jnp.arange(ranges, dtype=jnp.int32)]
    bit = ranges // 2
    while bit:
        asked = asked.reshape(ranges // (2 * bit), 2, bit, PMOST)
        moved = lax.ppermute(asked[:, 1], "ctx", [(i, i ^ bit) for i in range(ranges)])
        asked = jnp.stack([asked[:, 0], moved], axis=1).reshape(ranges, PMOST)
        bit //= 2
    asked = asked[own ^ jnp.arange(ranges, dtype=jnp.int32)]
    send = pack_first(key, value, query, steps, kv_per, 1)
    first = across(send, "head").reshape(-1, BLK, LANES)
    send_rest = pack_rest(query, 1, per)
    picked = pick_blocks(first, place(asked).reshape(-1))
    remote = across(picked.reshape(ranges, PMOST * BLK, LANES), "ctx")
    q_first = take_queries(first, sources * per)
    send_rest, remote, q_first = lax.optimization_barrier((send_rest, remote, q_first))
    table = put_remote(first, remote.reshape(-1, BLK, LANES), sources * per)
    q_rest = across(send_rest, "head").reshape(-1, BLK, LANES)

    out = None
    for c, q_pairs in enumerate((q_first, q_rest)):
        o_pairs = attend(table_index, q_pairs, table, sources, per, half * c, per_source)
        o_pairs = across(o_pairs.reshape(sources, per, BLK, LANES), "head")
        out = unpack(o_pairs, tok, width, per * c, out)
    return out


def solution(mesh):
    placed = (
        P(("ctx", "head"), None),
        P(("ctx", "head"), None),
        P(("ctx", "head"), None),
        P("head", "ctx", None),
    )
    return jax.shard_map(
        on_device,
        mesh=mesh,
        in_specs=placed,
        out_specs=P(("ctx", "head"), None),
        check_vma=False,
    )
```
